32 devices in a mesh: px: 16 (over z, x, core), py: 2 (over y).
Axes of the slice: x: 2, y: 2, z: 4, core: 2. Of those that a mesh axis runs over, the one named last changes fastest.
Arguments:
- table: float32 [25, 50, 1000], replicated, may hold values from -1 to 1
- charge: float32 [64, 8, 8], P('px', 'py'), may hold values from 0.1 to 1
- hit_bins: int32 [64, 8, 8], P('px', 'py'), may hold values from 0 to 49
- hit_ticks: int32 [64, 8, 8], P('px', 'py'), may hold values from 0 to 23
- active: int32 [64, 8], P('px', 'py'), may hold values 0 or 1
- measured: bfloat16 [64, 8, 1024], P('px', 'py'), may hold values from -6 to 6
- row_module: int32 [64], replicated, may hold values from 0 to 6, as said below
- col_module: int32 [8], replicated, may hold values from 0 to 4, as said below
Outputs:
- current: bfloat16 [64, 8, 1024], P('px', 'py')
- table_grad: float32 [25, 50, 1000], P(None, None, 'py')
The draws below stay inside these ranges and needn't reach their ends.
Inputs may be any that keep to these rules, and one draw needn't show every extreme that they name: `row_module`: starts at 0 and never falls; it rises by one at 6 rows. `col_module`: starts at 0 and never falls; it rises by one at 4 columns.
All inputs are finite; a program needn't handle non-finite values. No bound on the sum of `active` on one device may be relied on, other than what follows from the above.
Results may differ from the reference program's by a relative error of at most 0.014.
Values may be sent and summed in bfloat16 or wider, within the bound.
A program may use at most 128 MiB of HBM per device.

```python
import math
import jax
import jax.numpy as jnp
from jax import lax

BINS = 50
OFFS = 25
TICKS = 1000
SHIFTS = 24
HITS = 8
MOD_ROWS = 7
MOD_COLS = 5
TILE_X = 4
TILE_Y = 4
NX = 64
NY = 8
WAVE = 1024


def draw_hit_bins(key, part):
    rows = jnp.arange(NX, dtype=jnp.int32)[:, None, None] // TILE_X
    cols = jnp.arange(NY, dtype=jnp.int32)[None, :, None] // TILE_Y
    tile_id = rows * (NY // TILE_Y) + cols
    jitter = jax.random.randint(jax.random.fold_in(key, 5), (NX, NY, HITS), 0, 3, dtype=jnp.int32)
    nearby = (tile_id * 7 + jitter) % BINS
    spread = jax.random.randint(jax.random.fold_in(key, 6), (NX, NY, HITS), 0, BINS, dtype=jnp.int32)
    picker = jax.random.randint(jax.random.fold_in(key, 7), (NX, NY, HITS), 0, 2, dtype=jnp.int32)
    return jnp.where(picker == 1, nearby, spread).astype(jnp.int32)


def module_ids(key, count, pieces):
    starts = jax.random.permutation(key, count - 1)[:pieces - 1] + 1
    where_row = jnp.arange(count, dtype=jnp.int32)[:, None]
    return jnp.sum((starts[None, :] <= where_row).astype(jnp.int32), axis=1).astype(jnp.int32)


def draw_row_module(key, part):
    return module_ids(jax.random.fold_in(key, 11), NX, MOD_ROWS)


def draw_col_module(key, part):
    return module_ids(jax.random.fold_in(key, 13), NY, MOD_COLS)


def with_ends(result, own_key, smallest, top_value):
    place = [jax.random.randint(jax.random.fold_in(own_key, axis), (), 0, length) for axis, length in enumerate(result.shape)]
    main_axis = result.shape.index(max(result.shape))
    neighbour = place[:main_axis] + [(place[main_axis] + 1) % result.shape[main_axis]] + place[main_axis + 1:]
    return result.at[tuple(place)].set(smallest).at[tuple(neighbour)].set(top_value)


def block_scale(stream_key, dims, cuts, low, high):
    def one(axis_at, blocks):
        heights = jax.random.uniform(jax.random.fold_in(jax.random.fold_in(stream_key, 6), axis_at), (blocks,), jnp.float32, low / len(cuts), high / len(cuts))
        return jnp.repeat(jnp.exp(heights), dims[axis_at] // blocks).reshape((-1,) + (1,) * (len(dims) - axis_at - 1))

    gain = one(*cuts[0])
    for cut in cuts[1:]:
        gain = gain * one(*cut)
    return gain


def centred(stream_key, shape, scale, bound, cuts=(), held_as=jnp.bfloat16):
    drawn = scale * jax.random.normal(stream_key, shape, jnp.float32)
    if cuts:
        drawn = drawn * block_scale(stream_key, shape, cuts, -0.22, 0.18)
    return jnp.clip(drawn, -bound, bound).astype(held_as)


def setup_inputs(seed: int = 0) -> dict:
    keys = jax.random.split(jax.random.key(seed), 9)
    return {
        "table": centred(keys[0], (OFFS, BINS, TICKS), 0.15, 1.0, (), jnp.float32),
        "charge": jnp.clip(jnp.exp(math.log(1.0) - 2.3025851 * jax.random.uniform(keys[1], (NX, NY, HITS), jnp.float32) ** block_scale(keys[1], (NX, NY, HITS), ((0, 16), (1, 2)), -0.2, 0.2)), 0.1, 1.0),
        "hit_bins": draw_hit_bins(jax.random.fold_in(keys[8], 71), 0),
        "hit_ticks": with_ends(jax.random.randint(keys[3], (NX, NY, HITS), 0, SHIFTS), jax.random.fold_in(keys[3], 1), 0, SHIFTS - 1).astype(jnp.int32),
        "active": with_ends((jax.random.randint(keys[4], (NX, NY), 0, 4) < 3).astype(jnp.int32), jax.random.fold_in(keys[4], 1), 0, 1),
        "measured": centred(keys[5], (NX, NY, WAVE), 1.0, 6.0, ((0, 16), (1, 2))),
        "row_module": draw_row_module(jax.random.fold_in(keys[8], 71), 0),
        "col_module": draw_col_module(jax.random.fold_in(keys[8], 71), 0),
    }


def bin_charges(charge, hit_bins, hit_ticks):
    tick_hot = (hit_ticks[..., None] == jnp.arange(SHIFTS, dtype=jnp.int32)).astype(jnp.float32)
    bin_hot = (hit_bins[..., None] == jnp.arange(BINS, dtype=jnp.int32)).astype(jnp.float32)
    weighted = charge.astype(jnp.float32)[..., None] * tick_hot
    return jnp.einsum('xyks,xykb->xysb', weighted, bin_hot).astype(jnp.bfloat16)


def gather_offsets(source, rows, cols, count_x, count_y):
    pieces = []
    for row_off in range(-2, 3):
        for col_off in range(-2, 3):
            partial_value = source[2 - row_off:2 - row_off + count_x, 2 - col_off:2 - col_off + count_y]
            row_same = rows[2 - row_off:2 - row_off + count_x] == rows[2:2 + count_x]
            col_same = cols[2 - col_off:2 - col_off + count_y] == cols[2:2 + count_y]
            allowed = row_same[:, None] & col_same[None, :]
            pieces.append(jnp.where(allowed[:, :, None, None], partial_value, jnp.zeros((), partial_value.dtype)))
    return jnp.stack(pieces, 0)


def shift_sum(partial_value):
    total = jnp.zeros(partial_value.shape[:2] + (TICKS + SHIFTS,), jnp.float32)
    for offset in range(SHIFTS):
        total = total + jnp.pad(partial_value[:, :, offset, :], ((0, 0), (0, 0), (offset, SHIFTS - offset)))
    return total


def windows(resid):
    return jnp.stack([resid[:, :, offset:offset + TICKS] for offset in range(SHIFTS)], axis=2)


def reference(table, charge, hit_bins, hit_ticks, active, measured, row_module, col_module):
    binned = bin_charges(charge, hit_bins, hit_ticks)
    weights = lax.optimization_barrier(table.astype(jnp.bfloat16)).astype(jnp.float32)
    padded = jnp.pad(binned, ((2, 2), (2, 2), (0, 0), (0, 0)))
    rows_pad = jnp.pad(row_module, 2, constant_values=-1)
    cols_pad = jnp.pad(col_module, 2, constant_values=-1)

    def band(carry, index):
        start = index * TILE_X
        source = lax.dynamic_slice_in_dim(padded, start, TILE_X + 4, 0)
        rows = lax.dynamic_slice_in_dim(rows_pad, start, TILE_X + 4, 0)
        stacked = gather_offsets(source, rows, cols_pad, TILE_X, NY).astype(jnp.float32)
        partial_value = jnp.einsum('oxysb,obt->xyst', stacked, weights)
        prediction = shift_sum(partial_value)
        seen = lax.dynamic_slice_in_dim(measured, start, TILE_X, 0).astype(jnp.float32)
        reads = lax.dynamic_slice_in_dim(active, start, TILE_X, 0).astype(jnp.float32)
        resid = ((prediction - seen) * reads[..., None]).astype(jnp.bfloat16)
        contrib = jnp.einsum('oxysb,xysu->obu', stacked, windows(resid).astype(jnp.float32))
        return carry + contrib, prediction.astype(jnp.bfloat16)

    initial = jnp.zeros((OFFS, BINS, TICKS), jnp.float32)
    gradient, bands = lax.scan(band, initial, jnp.arange(NX // TILE_X, dtype=jnp.int32))
    current = bands.reshape(NX, NY, TICKS + SHIFTS)
    return current, gradient / (TILE_X * TILE_Y)
```

```python
import functools

import jax
import jax.numpy as jnp
from jax import lax
from jax.experimental import pallas as pl
from jax.experimental.pallas import tpu as pltpu
from jax.sharding import PartitionSpec as P

BINS = 50
SHIFTS = 24
REACH = 2
SPAN = 2 * REACH + 1
ROWS = 64
VMEM_BYTES = 48 * 1024 * 1024


def hot_rows(cc, hits, wide):
    bins = (lax.broadcasted_iota(jnp.int32, (ROWS, wide), 0) * SHIFTS).astype(jnp.float32)
    total = jnp.zeros((ROWS, wide), jnp.float32)
    for k in range(hits):
        code = jnp.broadcast_to(cc[k : k + 1], (ROWS, wide))
        load = jnp.broadcast_to(cc[hits + k : hits + k + 1], (ROWS, wide))
        total = jnp.where(code == bins, load, total)
    return total


def forward_kernel(hits, pixels, share, windows, cc_ref, table_ref, measured_ref, active_ref,
                   current_ref, window_ref, lhs, rhs):
    step = pl.program_id(0)
    wide = cc_ref.shape[2]
    ticks = table_ref.shape[2]
    wave = measured_ref.shape[1]
    for at in range(SPAN):
        hot = jnp.concatenate(
            [hot_rows(cc_ref[at, :, c : c + 128], hits, 128) for c in range(0, wide, 128)], axis=1
        )
        row = pl.multiple_of(step * (SPAN * ROWS) + at * ROWS, ROWS)
        lhs[pl.ds(row, ROWS), :] = hot.astype(jnp.bfloat16)
        weights = jnp.pad(table_ref[at], ((0, ROWS - BINS), (0, wave - ticks)))
        rhs[pl.ds(row, ROWS), :] = weights.astype(jnp.bfloat16)

    @pl.when(step == SPAN - 1)
    def _():
        spread = lax.dot_general(
            lhs[...], rhs[...], (((0,), (0,)), ((), ())), preferred_element_type=jnp.float32
        )
        total = spread[:pixels]
        for s in range(1, SHIFTS):
            total = total + pltpu.roll(spread[s * pixels : (s + 1) * pixels], s, axis=1)
        current_ref[...] = total.astype(jnp.bfloat16)
        resid = (total - measured_ref[...].astype(jnp.float32)) * active_ref[...]
        resid = resid.astype(jnp.bfloat16).astype(jnp.float32)
        reach = window_ref.shape[2]
        longer = jnp.pad(resid, ((0, 0), (0, reach)))
        length = longer.shape[1]
        for t in range(windows):
            moved = longer if t == 0 else pltpu.roll(longer, length - t * share, axis=1)
            window_ref[t] = moved[:, :reach].astype(jnp.bfloat16)


def backward_kernel(hits, scale, cols_ref, cc_ref, mask_ref, resid_ref, out_ref, lhs, rhs, acc):
    step = pl.program_id(0)
    wide = cc_ref.shape[2]
    count = resid_ref.shape[1]
    ticks = rhs.shape[2]
    slot = lax.rem(step, REACH + 1)

    @pl.when(step == 0)
    def _():
        acc[...] = jnp.zeros_like(acc)

    hot = jnp.concatenate(
        [hot_rows(cc_ref[0, :, c : c + 128], hits, 128) for c in range(0, wide, 128)], axis=1
    )
    for at in range(SPAN):
        moved = hot if at == REACH else pltpu.roll(hot, (at - REACH) % wide, axis=1)
        lhs[slot, at * ROWS : (at + 1) * ROWS, :] = (moved * mask_ref[at : at + 1]).astype(jnp.bfloat16)
    resid = resid_ref[0]
    for s in range(SHIFTS):
        rhs[slot, s * count : (s + 1) * count, :] = resid[:, s : s + ticks]

    def add(j, left, right):
        acc[j + REACH] += jnp.dot(lhs[left], rhs[right], preferred_element_type=jnp.float32)

    add(0, slot, slot)
    for back in range(1, REACH + 1):
        other = lax.rem(step + (REACH + 1) - back, REACH + 1)
        before = jnp.maximum(step - back, 0)

        @pl.when((step >= back) & (cols_ref[step] == cols_ref[before]))
        def _():
            add(-back, slot, other)
            add(back, other, slot)

    @pl.when(step == pl.num_programs(0) - 1)
    def _():
        for i in range(SPAN):
            for j in range(SPAN):
                part = acc[j, i * ROWS : i * ROWS + BINS, :]
                out_ref[i * SPAN + j] = part[:, : out_ref.shape[2]] * scale


def first_of(charge, hit_bins, hit_ticks):
    code = hit_bins * SHIFTS + hit_ticks
    same = code[..., :, None] == code[..., None, :]
    total = jnp.sum(jnp.where(same, charge[..., None, :], 0.0), axis=-1)
    hits = code.shape[-1]
    earlier = jnp.tril(jnp.ones((hits, hits), jnp.bool_), -1)
    first = ~jnp.any(same & earlier, axis=-1)
    code = jnp.where(first, code, -1).astype(jnp.float32)
    return jnp.concatenate([code, total.astype(jnp.bfloat16).astype(jnp.float32)], axis=-1)


def along_ticks(codes, hits):
    lanes = jnp.broadcast_to(codes[:, :, None, :], codes.shape[:2] + (SHIFTS, codes.shape[2]))
    ticks = jnp.arange(SHIFTS, dtype=jnp.float32)[:, None]
    is_code = (jnp.arange(2 * hits) < hits)[:, None, None]
    lanes = jnp.where(is_code, lanes - ticks, lanes)
    return lanes.reshape(codes.shape[0], codes.shape[1], SHIFTS * codes.shape[2])


def on_device(table, charge, hit_bins, hit_ticks, active, measured, row_module, col_module):
    tile_x, tile_y, hits = charge.shape
    pixels = tile_x * tile_y
    ticks = table.shape[2]
    wave = measured.shape[2]
    over_x, over_y = lax.axis_size("px"), lax.axis_size("py")
    rows, cols = tile_x * over_x, tile_y * over_y
    share = ticks // over_y
    ticks_wide = -(-share // 128) * 128
    reach = ticks_wide + 128

    packed = first_of(charge, hit_bins, hit_ticks)
    held = lax.all_gather(packed, ("px", "py"))
    held = held.reshape(over_x, over_y, tile_x, tile_y, 2 * hits)
    plane = held.transpose(0, 2, 1, 3, 4).reshape(rows, cols, 2 * hits)

    row_start = lax.axis_index("px") * tile_x
    col_start = lax.axis_index("py") * tile_y
    near = lax.dynamic_slice(
        jnp.pad(plane, ((REACH, REACH), (REACH, REACH), (0, 0)), constant_values=-1.0),
        (row_start, col_start, 0),
        (tile_x + 2 * REACH, tile_y + 2 * REACH, 2 * hits),
    )
    rows_pad = jnp.pad(row_module, REACH, constant_values=-1)
    cols_pad = jnp.pad(col_module, REACH, constant_values=-1)
    rows_near = lax.dynamic_slice_in_dim(rows_pad, row_start, tile_x + 2 * REACH, 0)
    cols_near = lax.dynamic_slice_in_dim(cols_pad, col_start, tile_y + 2 * REACH, 0)
    pieces = []
    for i in range(-REACH, REACH + 1):
        for j in range(-REACH, REACH + 1):
            at_x, at_y = slice(REACH - i, REACH - i + tile_x), slice(REACH - j, REACH - j + tile_y)
            row_same = rows_near[at_x] == rows_near[REACH : REACH + tile_x]
            col_same = cols_near[at_y] == cols_near[REACH : REACH + tile_y]
            allowed = row_same[:, None] & col_same[None, :]
            pieces.append(jnp.where(allowed[..., None], near[at_x, at_y], -1.0))
    sources = jnp.stack(pieces, 0).reshape(SPAN * SPAN, pixels, 2 * hits).transpose(0, 2, 1)
    sources = along_ticks(sources, hits)

    current, window = pl.pallas_call(
        functools.partial(forward_kernel, hits, pixels, share, over_y),
        grid=(SPAN,),
        in_specs=[
            pl.BlockSpec((SPAN, 2 * hits, SHIFTS * pixels), lambda g: (g, 0, 0)),
            pl.BlockSpec((SPAN, BINS, ticks), lambda g: (g, 0, 0)),
            pl.BlockSpec((pixels, wave), lambda g: (0, 0)),
            pl.BlockSpec((pixels, 1), lambda g: (0, 0)),
        ],
        out_specs=[
            pl.BlockSpec((pixels, wave), lambda g: (0, 0)),
            pl.BlockSpec((over_y, pixels, reach), lambda g: (0, 0, 0)),
        ],
        out_shape=[
            jax.ShapeDtypeStruct((pixels, wave), jnp.bfloat16),
            jax.ShapeDtypeStruct((over_y, pixels, reach), jnp.bfloat16),
        ],
        scratch_shapes=[
            pltpu.VMEM((SPAN * SPAN * ROWS, SHIFTS * pixels), jnp.bfloat16),
            pltpu.VMEM((SPAN * SPAN * ROWS, wave), jnp.bfloat16),
        ],
        compiler_params=pltpu.CompilerParams(vmem_limit_bytes=VMEM_BYTES),
        name="forward",
    )(
        sources,
        table,
        measured.reshape(pixels, wave),
        active.astype(jnp.float32).reshape(pixels, 1),
    )

    by_y = lax.all_to_all(window, "py", 0, 0)
    everyone = lax.all_gather(by_y, "px")
    everyone = everyone.reshape(over_x, over_y, tile_x, tile_y, reach)
    everyone = everyone.transpose(1, 3, 0, 2, 4).reshape(cols, rows, reach)

    columns = along_ticks(plane.transpose(1, 2, 0), hits)
    source_row = [
        lax.slice_in_dim(rows_pad, REACH - i, REACH - i + rows) for i in range(-REACH, REACH + 1)
    ]
    row_mask = jnp.stack([(r == row_module).astype(jnp.float32) for r in source_row], 0)
    row_mask = jnp.tile(jnp.pad(row_mask, ((0, 8 - SPAN), (0, 0))), (1, SHIFTS))

    gradient = pl.pallas_call(
        functools.partial(backward_kernel, hits, 1.0 / pixels),
        grid_spec=pltpu.PrefetchScalarGridSpec(
            num_scalar_prefetch=1,
            grid=(cols,),
            in_specs=[
                pl.BlockSpec((1, 2 * hits, SHIFTS * rows), lambda y, c: (y, 0, 0)),
                pl.BlockSpec((8, SHIFTS * rows), lambda y, c: (0, 0)),
                pl.BlockSpec((1, rows, reach), lambda y, c: (y, 0, 0)),
            ],
            out_specs=pl.BlockSpec((SPAN * SPAN, BINS, share), lambda y, c: (0, 0, 0)),
            scratch_shapes=[
                pltpu.VMEM((REACH + 1, SPAN * ROWS, SHIFTS * rows), jnp.bfloat16),
                pltpu.VMEM((REACH + 1, SHIFTS * rows, ticks_wide), jnp.bfloat16),
                pltpu.VMEM((SPAN, SPAN * ROWS, ticks_wide), jnp.float32),
            ],
        ),
        out_shape=jax.ShapeDtypeStruct((SPAN * SPAN, BINS, share), jnp.float32),
        compiler_params=pltpu.CompilerParams(vmem_limit_bytes=VMEM_BYTES),
        name="backward",
    )(col_module, columns, row_mask, everyone)
    return current.reshape(tile_x, tile_y, wave), gradient


def solution(mesh):
    in_specs = (
        P(),
        P("px", "py", None),
        P("px", "py", None),
        P("px", "py", None),
        P("px", "py"),
        P("px", "py", None),
        P(),
        P(),
    )
    out_specs = (P("px", "py", None), P(None, None, "py"))
    return jax.shard_map(
        on_device, mesh=mesh, in_specs=in_specs, out_specs=out_specs, check_vma=False
    )
```

```python
import functools

import jax
import jax.numpy as jnp
from jax import lax
from jax.experimental import pallas as pl
from jax.experimental.pallas import tpu as pltpu
from jax.sharding import PartitionSpec as P

BINS = 50
SHIFTS = 24
REACH = 2
SPAN = 2 * REACH + 1
ROWS = 64
VMEM_BYTES = 48 * 1024 * 1024


def hot_rows(cc, hits, first_tick):
    lanes = cc.shape[1]
    bins = (lax.broadcasted_iota(jnp.int32, (ROWS, lanes), 0) * SHIFTS).astype(jnp.float32)
    total = jnp.zeros((ROWS, lanes), jnp.float32)
    for k in range(hits):
        code = jnp.broadcast_to(cc[k : k + 1] - first_tick, (ROWS, lanes))
        load = jnp.broadcast_to(cc[hits + k : hits + k + 1], (ROWS, lanes))
        total = jnp.where(code == bins, load, total)
    return total


def gather_kernel(source_ref, out_ref, own_sem, send_sem, recv_sem, on_sem, pass_sem):
    over_x, over_y = out_ref.shape[0], out_ref.shape[1]
    me_x, me_y = lax.axis_index("px"), lax.axis_index("py")
    core = lax.rem(me_x, 2)
    beside = me_x + 1 - 2 * core
    chips = (over_x // 2) * over_y
    here = (me_x // 2) * over_y + me_y

    def place(chip):
        return (chip // over_y) * 2 + core, lax.rem(chip, over_y)

    barrier = pltpu.get_barrier_semaphore()

    @pl.loop(1, chips)
    def _(d):
        pl.semaphore_signal(barrier, inc=1, device_id=place(lax.rem(here + d, chips)),
                            device_id_type=pl.DeviceIdType.MESH)

    pl.semaphore_signal(barrier, inc=1, device_id=(beside, me_y),
                        device_id_type=pl.DeviceIdType.MESH)
    own = pltpu.make_async_copy(source_ref.at[lax.rem(me_y, source_ref.shape[0])],
                                out_ref.at[me_x, me_y], own_sem)
    own.start()
    pl.semaphore_wait(barrier, chips)

    def send(d):
        x, y = place(lax.rem(here + d, chips))
        return pltpu.make_async_remote_copy(
            src_ref=source_ref.at[lax.rem(y, source_ref.shape[0])],
            dst_ref=out_ref.at[me_x, me_y],
            send_sem=send_sem.at[d],
            recv_sem=recv_sem.at[d],
            device_id=(x, y),
            device_id_type=pl.DeviceIdType.MESH,
        )

    def hand_on(d, source):
        x, y = place(lax.rem(here + chips - d, chips))
        return pltpu.make_async_remote_copy(
            src_ref=source,
            dst_ref=out_ref.at[x, y],
            send_sem=on_sem.at[d],
            recv_sem=pass_sem.at[d],
            device_id=(beside, me_y),
            device_id_type=pl.DeviceIdType.MESH,
        )

    def arrived(d):
        x, y = place(lax.rem(here + chips - d, chips))
        return out_ref.at[x, y]

    mine = source_ref.at[lax.rem(me_y, source_ref.shape[0])]

    @pl.loop(1, chips)
    def _(d):
        send(d).start()

    hand_on(0, mine).start()

    @pl.loop(1, chips)
    def _(d):
        send(d).wait_recv()
        hand_on(d, arrived(d)).start()

    hand_on(0, mine).wait()

    @pl.loop(1, chips)
    def _(d):
        send(d).wait_send()
        hand_on(d, arrived(d)).wait()

    own.wait()


def everywhere(blocks, over_x, over_y, number, name):
    chips = (over_x // 2) * over_y
    return pl.pallas_call(
        gather_kernel,
        in_specs=[pl.BlockSpec(memory_space=pltpu.VMEM)],
        out_specs=pl.BlockSpec(memory_space=pltpu.VMEM),
        out_shape=jax.ShapeDtypeStruct((over_x, over_y) + blocks.shape[1:], blocks.dtype),
        scratch_shapes=[pltpu.SemaphoreType.DMA] + [pltpu.SemaphoreType.DMA((chips,))] * 4,
        compiler_params=pltpu.CompilerParams(
            collective_id=number, has_side_effects=True, vmem_limit_bytes=VMEM_BYTES
        ),
        name=name,
    )(blocks)


def forward_kernel(hits, pixels, share, windows, cc_ref, table_ref, measured_ref, active_ref,
                   current_ref, window_ref, lhs, rhs):
    step = pl.program_id(0)
    lanes = cc_ref.shape[2]
    wide = SHIFTS * pixels
    ticks = table_ref.shape[2]
    wave = measured_ref.shape[1]
    for at in range(SPAN):
        cc = cc_ref[at]
        row = pl.multiple_of(step * (SPAN * ROWS) + at * ROWS, ROWS)
        for c in range(0, wide, lanes):
            hot = hot_rows(cc, hits, float(c // pixels))
            lhs[pl.ds(row, ROWS), c : c + lanes] = hot.astype(jnp.bfloat16)
        weights = jnp.pad(table_ref[at], ((0, ROWS - BINS), (0, wave - ticks)))
        rhs[pl.ds(row, ROWS), :] = weights.astype(jnp.bfloat16)

    @pl.when(step == SPAN - 1)
    def _():
        spread = lax.dot_general(
            lhs[...], rhs[...], (((0,), (0,)), ((), ())), preferred_element_type=jnp.float32
        )
        total = spread[:pixels]
        for s in range(1, SHIFTS):
            total = total + pltpu.roll(spread[s * pixels : (s + 1) * pixels], s, axis=1)
        current_ref[...] = total.astype(jnp.bfloat16)
        resid = (total - measured_ref[...].astype(jnp.float32)) * active_ref[...]
        resid = resid.astype(jnp.bfloat16).astype(jnp.float32)
        reach = window_ref.shape[2]
        longer = jnp.pad(resid, ((0, 0), (0, reach)))
        length = longer.shape[1]
        for t in range(windows):
            moved = longer if t == 0 else pltpu.roll(longer, length - t * share, axis=1)
            window_ref[t] = moved[:, :reach].astype(jnp.bfloat16)


def backward_kernel(hits, scale, cols_ref, cc_ref, mask_ref, resid_ref, out_ref, lhs, rhs, acc):
    step = pl.program_id(0)
    lanes = cc_ref.shape[2]
    count = resid_ref.shape[1]
    wide = SHIFTS * count
    ticks = rhs.shape[2]
    slot = lax.rem(step, REACH + 1)

    @pl.when(step == 0)
    def _():
        acc[...] = jnp.zeros_like(acc)

    cc = cc_ref[0]
    for c in range(0, wide, lanes):
        hot = hot_rows(cc, hits, float(c // count))
        for at in range(SPAN):
            moved = hot if at == REACH else pltpu.roll(hot, (at - REACH) % lanes, axis=1)
            lhs[slot, at * ROWS : (at + 1) * ROWS, c : c + lanes] = (
                moved * mask_ref[at : at + 1]
            ).astype(jnp.bfloat16)
    resid = resid_ref[0]
    for s in range(SHIFTS):
        rhs[slot, s * count : (s + 1) * count, :] = resid[:, s : s + ticks]

    def add(j, left, right):
        acc[j + REACH] += jnp.dot(lhs[left], rhs[right], preferred_element_type=jnp.float32)

    add(0, slot, slot)
    for back in range(1, REACH + 1):
        other = lax.rem(step + (REACH + 1) - back, REACH + 1)
        before = jnp.maximum(step - back, 0)

        @pl.when((step >= back) & (cols_ref[step] == cols_ref[before]))
        def _():
            add(-back, slot, other)
            add(back, other, slot)

    @pl.when(step == pl.num_programs(0) - 1)
    def _():
        for i in range(SPAN):
            for j in range(SPAN):
                part = acc[j, i * ROWS : i * ROWS + BINS, :]
                out_ref[i * SPAN + j] = part[:, : out_ref.shape[2]] * scale


def first_of(charge, hit_bins, hit_ticks):
    code = hit_bins * SHIFTS + hit_ticks
    same = code[..., :, None] == code[..., None, :]
    total = jnp.sum(jnp.where(same, charge[..., None, :], 0.0), axis=-1)
    hits = code.shape[-1]
    earlier = jnp.tril(jnp.ones((hits, hits), jnp.bool_), -1)
    first = ~jnp.any(same & earlier, axis=-1)
    code = jnp.where(first, code, -1).astype(jnp.float32)
    return jnp.concatenate([code, total.astype(jnp.bfloat16).astype(jnp.float32)], axis=-1)


def along_ticks(codes, hits):
    count = codes.shape[2]
    ticks = max(1, 128 // count)
    lanes = jnp.broadcast_to(codes[:, :, None, :], codes.shape[:2] + (ticks, count))
    after = jnp.arange(ticks, dtype=jnp.float32)[:, None]
    is_code = (jnp.arange(2 * hits) < hits)[:, None, None]
    lanes = jnp.where(is_code, lanes - after, lanes)
    return lanes.reshape(codes.shape[0], codes.shape[1], ticks * count)


def on_device(table, charge, hit_bins, hit_ticks, active, measured, row_module, col_module):
    tile_x, tile_y, hits = charge.shape
    pixels = tile_x * tile_y
    ticks = table.shape[2]
    wave = measured.shape[2]
    over_x, over_y = lax.axis_size("px"), lax.axis_size("py")
    rows, cols = tile_x * over_x, tile_y * over_y
    share = ticks // over_y
    ticks_wide = -(-share // 128) * 128
    reach = ticks_wide + 128

    packed = first_of(charge, hit_bins, hit_ticks)
    held = everywhere(packed.reshape(1, -1, 128), over_x, over_y, 0, "deposits")
    held = held.reshape(over_x, over_y, tile_x, tile_y, 2 * hits)
    plane = held.transpose(0, 2, 1, 3, 4).reshape(rows, cols, 2 * hits)

    row_start = lax.axis_index("px") * tile_x
    col_start = lax.axis_index("py") * tile_y
    near = lax.dynamic_slice(
        jnp.pad(plane, ((REACH, REACH), (REACH, REACH), (0, 0)), constant_values=-1.0),
        (row_start, col_start, 0),
        (tile_x + 2 * REACH, tile_y + 2 * REACH, 2 * hits),
    )
    rows_pad = jnp.pad(row_module, REACH, constant_values=-1)
    cols_pad = jnp.pad(col_module, REACH, constant_values=-1)
    rows_near = lax.dynamic_slice_in_dim(rows_pad, row_start, tile_x + 2 * REACH, 0)
    cols_near = lax.dynamic_slice_in_dim(cols_pad, col_start, tile_y + 2 * REACH, 0)
    pieces = []
    for i in range(-REACH, REACH + 1):
        for j in range(-REACH, REACH + 1):
            at_x, at_y = slice(REACH - i, REACH - i + tile_x), slice(REACH - j, REACH - j + tile_y)
            row_same = rows_near[at_x] == rows_near[REACH : REACH + tile_x]
            col_same = cols_near[at_y] == cols_near[REACH : REACH + tile_y]
            allowed = row_same[:, None] & col_same[None, :]
            pieces.append(jnp.where(allowed[..., None], near[at_x, at_y], -1.0))
    sources = jnp.stack(pieces, 0).reshape(SPAN * SPAN, pixels, 2 * hits).transpose(0, 2, 1)
    sources = along_ticks(sources, hits)

    current, window = pl.pallas_call(
        functools.partial(forward_kernel, hits, pixels, share, over_y),
        grid=(SPAN,),
        in_specs=[
            pl.BlockSpec((SPAN, 2 * hits, sources.shape[2]), lambda g: (g, 0, 0)),
            pl.BlockSpec((SPAN, BINS, ticks), lambda g: (g, 0, 0)),
            pl.BlockSpec((pixels, wave), lambda g: (0, 0)),
            pl.BlockSpec((pixels, 1), lambda g: (0, 0)),
        ],
        out_specs=[
            pl.BlockSpec((pixels, wave), lambda g: (0, 0)),
            pl.BlockSpec((over_y, pixels, reach), lambda g: (0, 0, 0)),
        ],
        out_shape=[
            jax.ShapeDtypeStruct((pixels, wave), jnp.bfloat16),
            jax.ShapeDtypeStruct((over_y, pixels, reach), jnp.bfloat16),
        ],
        scratch_shapes=[
            pltpu.VMEM((SPAN * SPAN * ROWS, SHIFTS * pixels), jnp.bfloat16),
            pltpu.VMEM((SPAN * SPAN * ROWS, wave), jnp.bfloat16),
        ],
        compiler_params=pltpu.CompilerParams(vmem_limit_bytes=VMEM_BYTES),
        name="forward",
    )(
        sources,
        table,
        measured.reshape(pixels, wave),
        active.astype(jnp.float32).reshape(pixels, 1),
    )

    everyone = everywhere(window, over_x, over_y, 1, "residuals")
    everyone = everyone.reshape(over_x, over_y, tile_x, tile_y, reach)
    everyone = everyone.transpose(1, 3, 0, 2, 4).reshape(cols, rows, reach)

    columns = along_ticks(plane.transpose(1, 2, 0), hits)
    source_row = [
        lax.slice_in_dim(rows_pad, REACH - i, REACH - i + rows) for i in range(-REACH, REACH + 1)
    ]
    row_mask = jnp.stack([(r == row_module).astype(jnp.float32) for r in source_row], 0)
    row_mask = jnp.tile(jnp.pad(row_mask, ((0, 8 - SPAN), (0, 0))), (1, columns.shape[2] // rows))

    gradient = pl.pallas_call(
        functools.partial(backward_kernel, hits, 1.0 / pixels),
        grid_spec=pltpu.PrefetchScalarGridSpec(
            num_scalar_prefetch=1,
            grid=(cols,),
            in_specs=[
                pl.BlockSpec((1, 2 * hits, columns.shape[2]), lambda y, c: (y, 0, 0)),
                pl.BlockSpec((8, columns.shape[2]), lambda y, c: (0, 0)),
                pl.BlockSpec((1, rows, reach), lambda y, c: (y, 0, 0)),
            ],
            out_specs=pl.BlockSpec((SPAN * SPAN, BINS, share), lambda y, c: (0, 0, 0)),
            scratch_shapes=[
                pltpu.VMEM((REACH + 1, SPAN * ROWS, SHIFTS * rows), jnp.bfloat16),
                pltpu.VMEM((REACH + 1, SHIFTS * rows, ticks_wide), jnp.bfloat16),
                pltpu.VMEM((SPAN, SPAN * ROWS, ticks_wide), jnp.float32),
            ],
        ),
        out_shape=jax.ShapeDtypeStruct((SPAN * SPAN, BINS, share), jnp.float32),
        compiler_params=pltpu.CompilerParams(vmem_limit_bytes=VMEM_BYTES),
        name="backward",
    )(col_module, columns, row_mask, everyone)
    return current.reshape(tile_x, tile_y, wave), gradient


def solution(mesh):
    in_specs = (
        P(),
        P("px", "py", None),
        P("px", "py", None),
        P("px", "py", None),
        P("px", "py"),
        P("px", "py", None),
        P(),
        P(),
    )
    out_specs = (P("px", "py", None), P(None, None, "py"))
    return jax.shard_map(
        on_device, mesh=mesh, in_specs=in_specs, out_specs=out_specs, check_vma=False
    )
```

```python
import functools

import jax
import jax.numpy as jnp
from jax import lax
from jax.experimental import pallas as pl
from jax.experimental.pallas import tpu as pltpu
from jax.sharding import PartitionSpec as P

BINS = 50
SHIFTS = 24
REACH = 2
SPAN = 2 * REACH + 1
ROWS = 56
STACK = -(-SPAN * ROWS // 16) * 16
MIB = 1024 * 1024


def hot_rows(cc, hits, first_tick):
    lanes = cc.shape[1]
    bins = (lax.broadcasted_iota(jnp.int32, (ROWS, lanes), 0) * SHIFTS).astype(jnp.float32)
    total = jnp.zeros((ROWS, lanes), jnp.float32)
    for k in range(hits):
        code = jnp.broadcast_to(cc[k : k + 1] - first_tick, (ROWS, lanes))
        load = jnp.broadcast_to(cc[hits + k : hits + k + 1], (ROWS, lanes))
        total = jnp.where(code == bins, load, total)
    return total


def merged(cc, hits):
    code, load = cc[:hits], cc[hits:]
    row = lax.broadcasted_iota(jnp.int32, code.shape, 0)
    total, spent = load, jnp.zeros(code.shape, jnp.float32)
    for d in range(1, hits):
        same = code == pltpu.roll(code, d, axis=0)
        total = total + jnp.where(same, pltpu.roll(load, d, axis=0), 0.0)
        spent = jnp.where(same & (row >= d), 1.0, spent)
    return jnp.concatenate([jnp.where(spent > 0.0, -1000.0, code), total], axis=0)


def gather_kernel(source_ref, out_ref, own_sem, send_sem, recv_sem, on_sem, pass_sem):
    over_x, over_y = out_ref.shape[0], out_ref.shape[1]
    me_x, me_y = lax.axis_index("px"), lax.axis_index("py")
    core = lax.rem(me_x, 2)
    beside = me_x + 1 - 2 * core
    chips = (over_x // 2) * over_y
    here = (me_x // 2) * over_y + me_y

    def place(chip):
        return lax.div(chip, over_y) * 2 + core, lax.rem(chip, over_y)

    def after(d):
        chip = here + d
        return jnp.where(chip >= chips, chip - chips, chip)

    def ahead(d):
        chip = here - d
        return jnp.where(chip < 0, chip + chips, chip)

    unroll = chips - 1 if chips <= 16 else 1
    barrier = pltpu.get_barrier_semaphore()

    @pl.loop(1, chips, unroll=unroll)
    def _(d):
        pl.semaphore_signal(barrier, inc=1, device_id=place(after(d)),
                            device_id_type=pl.DeviceIdType.MESH)

    pl.semaphore_signal(barrier, inc=1, device_id=(beside, me_y),
                        device_id_type=pl.DeviceIdType.MESH)
    own = pltpu.make_async_copy(source_ref.at[lax.rem(me_y, source_ref.shape[0])],
                                out_ref.at[me_x, me_y], own_sem)
    own.start()
    pl.semaphore_wait(barrier, chips)

    def send(d):
        x, y = place(after(d))
        return pltpu.make_async_remote_copy(
            src_ref=source_ref.at[lax.rem(y, source_ref.shape[0])],
            dst_ref=out_ref.at[me_x, me_y],
            send_sem=send_sem.at[d],
            recv_sem=recv_sem.at[d],
            device_id=(x, y),
            device_id_type=pl.DeviceIdType.MESH,
        )

    def hand_on(d, source):
        x, y = place(ahead(d))
        return pltpu.make_async_remote_copy(
            src_ref=source,
            dst_ref=out_ref.at[x, y],
            send_sem=on_sem.at[d],
            recv_sem=pass_sem.at[d],
            device_id=(beside, me_y),
            device_id_type=pl.DeviceIdType.MESH,
        )

    def arrived(d):
        x, y = place(ahead(d))
        return out_ref.at[x, y]

    mine = source_ref.at[lax.rem(me_y, source_ref.shape[0])]

    @pl.loop(1, chips, unroll=unroll)
    def _(d):
        send(d).start()

    hand_on(0, mine).start()

    @pl.loop(1, chips, unroll=unroll)
    def _(d):
        send(d).wait_recv()
        hand_on(d, arrived(d)).start()

    hand_on(0, mine).wait()

    @pl.loop(1, chips, unroll=unroll)
    def _(d):
        send(d).wait_send()
        hand_on(d, arrived(d)).wait()

    own.wait()


def everywhere(blocks, over_x, over_y, number, room, name):
    chips = (over_x // 2) * over_y
    return pl.pallas_call(
        gather_kernel,
        in_specs=[pl.BlockSpec(memory_space=pltpu.VMEM)],
        out_specs=pl.BlockSpec(memory_space=pltpu.VMEM),
        out_shape=jax.ShapeDtypeStruct((over_x, over_y) + blocks.shape[1:], blocks.dtype),
        scratch_shapes=[pltpu.SemaphoreType.DMA] + [pltpu.SemaphoreType.DMA((chips,))] * 4,
        compiler_params=pltpu.CompilerParams(
            collective_id=number, has_side_effects=True, vmem_limit_bytes=room * MIB
        ),
        name=name,
    )(blocks)


def forward_kernel(hits, pixels, share, windows, cc_ref, table_ref, measured_ref, active_ref,
                   current_ref, window_ref, lhs, rhs):
    step = pl.program_id(0)
    lanes = cc_ref.shape[2]
    wide = SHIFTS * pixels
    ticks = table_ref.shape[2]
    wave = measured_ref.shape[1]
    first = pl.multiple_of(step * STACK, STACK)
    spare = STACK - SPAN * ROWS
    ccs = [merged(cc_ref[at], hits) for at in range(SPAN)]
    for c in range(0, wide, lanes):
        hot = [hot_rows(cc, hits, float(c // pixels)) for cc in ccs]
        hot = jnp.concatenate(hot + [jnp.zeros((spare, lanes), jnp.float32)], axis=0)
        lhs[pl.ds(first, STACK), c : c + lanes] = hot.astype(jnp.bfloat16)
    weights = [
        jnp.pad(table_ref[at], ((0, ROWS - BINS), (0, wave - ticks))) for at in range(SPAN)
    ]
    weights = jnp.concatenate(weights + [jnp.zeros((spare, wave), jnp.float32)], axis=0)
    rhs[pl.ds(first, STACK), :] = weights.astype(jnp.bfloat16)

    @pl.when(step == SPAN - 1)
    def _():
        spread = lax.dot_general(
            lhs[...], rhs[...], (((0,), (0,)), ((), ())), preferred_element_type=jnp.float32
        )
        total = spread[:pixels]
        for s in range(1, SHIFTS):
            total = total + pltpu.roll(spread[s * pixels : (s + 1) * pixels], s, axis=1)
        current_ref[...] = total.astype(jnp.bfloat16)
        resid = (total - measured_ref[...].astype(jnp.float32)) * active_ref[...]
        resid = resid.astype(jnp.bfloat16).astype(jnp.float32)
        reach = window_ref.shape[2]
        longer = jnp.pad(resid, ((0, 0), (0, reach)))
        length = longer.shape[1]
        for t in range(windows):
            moved = longer if t == 0 else pltpu.roll(longer, length - t * share, axis=1)
            window_ref[t] = moved[:, :reach].astype(jnp.bfloat16)


def backward_kernel(hits, scale, cols_ref, cc_ref, mask_ref, resid_ref, out_ref, lhs, rhs, acc):
    step = pl.program_id(0)
    lanes = cc_ref.shape[2]
    count = resid_ref.shape[1]
    wide = SHIFTS * count
    ticks = rhs.shape[2]
    slot = lax.rem(step, REACH + 1)

    @pl.when(step == 0)
    def _():
        acc[...] = jnp.zeros_like(acc)

    cc = merged(cc_ref[0], hits)
    spare = jnp.zeros((STACK - SPAN * ROWS, lanes), jnp.float32)
    for c in range(0, wide, lanes):
        hot = hot_rows(cc, hits, float(c // count))
        turned = [
            (hot if at == REACH else pltpu.roll(hot, (at - REACH) % lanes, axis=1))
            * mask_ref[at : at + 1]
            for at in range(SPAN)
        ]
        stacked = jnp.concatenate(turned + [spare], axis=0)
        lhs[slot, :, c : c + lanes] = stacked.astype(jnp.bfloat16)
    resid = resid_ref[0]
    for s in range(SHIFTS):
        rhs[slot, s * count : (s + 1) * count, :] = resid[:, s : s + ticks]

    def add(j, left, right):
        acc[j + REACH] += jnp.dot(lhs[left], rhs[right], preferred_element_type=jnp.float32)

    add(0, slot, slot)
    for back in range(1, REACH + 1):
        other = lax.rem(step + (REACH + 1) - back, REACH + 1)
        before = jnp.maximum(step - back, 0)

        @pl.when((step >= back) & (cols_ref[step] == cols_ref[before]))
        def _():
            add(-back, slot, other)
            add(back, other, slot)

    @pl.when(step == pl.num_programs(0) - 1)
    def _():
        for i in range(SPAN):
            for j in range(SPAN):
                part = acc[j, i * ROWS : i * ROWS + BINS, :]
                out_ref[i * SPAN + j] = part[:, : out_ref.shape[2]] * scale


def along_ticks(codes, hits):
    count = codes.shape[2]
    ticks = max(1, 128 // count)
    lanes = jnp.broadcast_to(codes[:, :, None, :], codes.shape[:2] + (ticks, count))
    after = jnp.arange(ticks, dtype=jnp.float32)[:, None]
    is_code = (jnp.arange(2 * hits) < hits)[:, None, None]
    lanes = jnp.where(is_code, lanes - after, lanes)
    return lanes.reshape(codes.shape[0], codes.shape[1], ticks * count)


def on_device(table, charge, hit_bins, hit_ticks, active, measured, row_module, col_module):
    tile_x, tile_y, hits = charge.shape
    pixels = tile_x * tile_y
    ticks = table.shape[2]
    wave = measured.shape[2]
    over_x, over_y = lax.axis_size("px"), lax.axis_size("py")
    rows, cols = tile_x * over_x, tile_y * over_y
    share = ticks // over_y
    ticks_wide = -(-share // 128) * 128
    reach = ticks_wide + 128

    packed = jnp.concatenate(
        [(hit_bins * SHIFTS + hit_ticks).astype(jnp.float32), charge], axis=-1
    )
    held = everywhere(packed.reshape(1, -1, 128), over_x, over_y, 0, 4, "deposits")
    held = held.reshape(over_x, over_y, tile_x, tile_y, 2 * hits)
    plane = held.transpose(0, 2, 1, 3, 4).reshape(rows, cols, 2 * hits)

    row_start = lax.axis_index("px") * tile_x
    col_start = lax.axis_index("py") * tile_y
    modules = jnp.stack(
        [
            jnp.broadcast_to(row_module[:, None], (rows, cols)),
            jnp.broadcast_to(col_module[None, :], (rows, cols)),
        ],
        axis=-1,
    ).astype(jnp.float32)
    near = lax.dynamic_slice(
        jnp.pad(
            jnp.concatenate([plane, modules], axis=-1),
            ((REACH, REACH), (REACH, REACH), (0, 0)),
            constant_values=-1.0,
        ),
        (row_start, col_start, 0),
        (tile_x + 2 * REACH, tile_y + 2 * REACH, 2 * hits + 2),
    )
    own = near[REACH : REACH + tile_x, REACH : REACH + tile_y, 2 * hits :]
    pieces = []
    for i in range(-REACH, REACH + 1):
        for j in range(-REACH, REACH + 1):
            piece = near[REACH - i : REACH - i + tile_x, REACH - j : REACH - j + tile_y]
            allowed = jnp.all(piece[..., 2 * hits :] == own, axis=-1, keepdims=True)
            pieces.append(jnp.where(allowed, piece[..., : 2 * hits], -1.0))
    rows_pad = jnp.pad(row_module, REACH, constant_values=-1)
    sources = jnp.stack(pieces, 0).reshape(SPAN * SPAN, pixels, 2 * hits).transpose(0, 2, 1)
    sources = along_ticks(sources, hits)

    current, window = pl.pallas_call(
        functools.partial(forward_kernel, hits, pixels, share, over_y),
        grid=(SPAN,),
        in_specs=[
            pl.BlockSpec((SPAN, 2 * hits, sources.shape[2]), lambda g: (g, 0, 0)),
            pl.BlockSpec((SPAN, BINS, ticks), lambda g: (g, 0, 0)),
            pl.BlockSpec((pixels, wave), lambda g: (0, 0)),
            pl.BlockSpec((pixels, 1), lambda g: (0, 0)),
        ],
        out_specs=[
            pl.BlockSpec((pixels, wave), lambda g: (0, 0)),
            pl.BlockSpec((over_y, pixels, reach), lambda g: (0, 0, 0)),
        ],
        out_shape=[
            jax.ShapeDtypeStruct((pixels, wave), jnp.bfloat16),
            jax.ShapeDtypeStruct((over_y, pixels, reach), jnp.bfloat16),
        ],
        scratch_shapes=[
            pltpu.VMEM((SPAN * STACK, SHIFTS * pixels), jnp.bfloat16),
            pltpu.VMEM((SPAN * STACK, wave), jnp.bfloat16),
        ],
        compiler_params=pltpu.CompilerParams(vmem_limit_bytes=60 * MIB),
        name="forward",
    )(
        sources,
        table,
        measured.reshape(pixels, wave),
        active.astype(jnp.float32).reshape(pixels, 1),
    )

    everyone = everywhere(window, over_x, over_y, 1, 24, "residuals")
    everyone = everyone.reshape(over_x, over_y, tile_x, tile_y, reach)
    everyone = everyone.transpose(1, 3, 0, 2, 4).reshape(cols, rows, reach)

    columns = along_ticks(plane.transpose(1, 2, 0), hits)
    source_row = [
        lax.slice_in_dim(rows_pad, REACH - i, REACH - i + rows) for i in range(-REACH, REACH + 1)
    ]
    row_mask = jnp.stack([(r == row_module).astype(jnp.float32) for r in source_row], 0)
    row_mask = jnp.tile(jnp.pad(row_mask, ((0, 8 - SPAN), (0, 0))), (1, columns.shape[2] // rows))

    gradient = pl.pallas_call(
        functools.partial(backward_kernel, hits, 1.0 / pixels),
        grid_spec=pltpu.PrefetchScalarGridSpec(
            num_scalar_prefetch=1,
            grid=(cols,),
            in_specs=[
                pl.BlockSpec((1, 2 * hits, columns.shape[2]), lambda y, c: (y, 0, 0)),
                pl.BlockSpec((8, columns.shape[2]), lambda y, c: (0, 0)),
                pl.BlockSpec((1, rows, reach), lambda y, c: (y, 0, 0)),
            ],
            out_specs=pl.BlockSpec((SPAN * SPAN, BINS, share), lambda y, c: (0, 0, 0)),
            scratch_shapes=[
                pltpu.VMEM((REACH + 1, STACK, SHIFTS * rows), jnp.bfloat16),
                pltpu.VMEM((REACH + 1, SHIFTS * rows, ticks_wide), jnp.bfloat16),
                pltpu.VMEM((SPAN, STACK, ticks_wide), jnp.float32),
            ],
        ),
        out_shape=jax.ShapeDtypeStruct((SPAN * SPAN, BINS, share), jnp.float32),
        compiler_params=pltpu.CompilerParams(vmem_limit_bytes=40 * MIB),
        name="backward",
    )(col_module, columns, row_mask, everyone)
    return current.reshape(tile_x, tile_y, wave), gradient


def solution(mesh):
    in_specs = (
        P(),
        P("px", "py", None),
        P("px", "py", None),
        P("px", "py", None),
        P("px", "py"),
        P("px", "py", None),
        P(),
        P(),
    )
    out_specs = (P("px", "py", None), P(None, None, "py"))
    return jax.shard_map(
        on_device, mesh=mesh, in_specs=in_specs, out_specs=out_specs, check_vma=False
    )
```
